256 devices in a mesh: row: 16 (over z, core), col: 16 (over x, y).
Axes of the slice: x: 4, y: 4, z: 8, core: 2. Of those that a mesh axis runs over, the one named last changes fastest.
Arguments:
- left_panel: bfloat16 [2, 16384, 1024], P(None, 'row', 'col'), may hold values from -0.125 to 0.125
- right_panel: bfloat16 [2, 1024, 16384], P(None, 'row', 'col'), may hold values from -6 to 6
Outputs:
- multiples: float32 [2, 16384, 16384], P(None, 'row', 'col')
The draws below stay inside these ranges and needn't reach their ends.
All inputs are finite; a program needn't handle non-finite values.
Results may differ from the reference program's by a relative error of at most 0.0003.
Values may be sent and summed in bfloat16 or wider, within the bound.
No kernel may reach another device: no remote copies, remote signals or barrier semaphores. Data moves between devices by JAX's collectives and lax.ppermute only.
A program may use at most 64 MiB of HBM per device.

```python
import jax
import jax.numpy as jnp

DEPTH = 1024
ROWS = 16384
COLS = 16384


def steps_of(rng, dims, cuts, smallest, largest):
    factor_of, own = 1.0, jax.random.fold_in(rng, 6)
    for dim, blocks in cuts:
        steps = jnp.exp(jax.random.uniform(jax.random.fold_in(own, dim), (blocks,), jnp.float32, smallest / len(cuts), largest / len(cuts)))
        factor_of = factor_of * jnp.repeat(steps, dims[dim] // blocks).reshape([-1 if axis == dim else 1 for axis in range(len(dims))])
    return factor_of


def gaussian(rng, extent, spread, most, cuts=(), kind=jnp.bfloat16):
    entries = spread * jax.random.normal(rng, extent, jnp.float32)
    if cuts:
        entries = entries * steps_of(rng, extent, cuts, -0.22, 0.18)
    return jnp.clip(entries, -most, most).astype(kind)


def setup_inputs(seed: int = 0) -> dict:
    key_list = jax.random.split(jax.random.key(seed), 3)
    return {
        "left_panel": gaussian(key_list[0], (2, ROWS, DEPTH), (2 * DEPTH) ** -0.5, 0.125, ((1, 16), (2, 16))),
        "right_panel": gaussian(key_list[1], (2, DEPTH, COLS), 1.0, 6.0, ((1, 16), (2, 16))),
    }


def reference(left_panel, right_panel):
    left_real, left_imag = left_panel[0], left_panel[1]
    right_real, right_imag = right_panel[0], right_panel[1]
    real_part = jnp.dot(left_real, right_real, preferred_element_type=jnp.float32) - jnp.dot(left_imag, right_imag, preferred_element_type=jnp.float32)
    imag_part = jnp.dot(left_real, right_imag, preferred_element_type=jnp.float32) + jnp.dot(left_imag, right_real, preferred_element_type=jnp.float32)
    return jnp.stack([real_part, imag_part])
```

```python
import jax
import jax.numpy as jnp
from jax import lax
from jax.experimental import pallas as pl
from jax.experimental.pallas import tpu as pltpu
from jax.sharding import PartitionSpec as P

AXES = ("row", "col")
RING = (0, -1, 1, 2)


def permute(value, target):
    pairs = []
    for z in range(8):
        for core in range(2):
            for x in range(4):
                for y in range(4):
                    to_z, to_core, to_x, to_y = target(z, core, x, y)
                    pairs.append(
                        (
                            (z * 2 + core) * 16 + x * 4 + y,
                            (to_z % 8 * 2 + to_core) * 16 + to_x % 4 * 4 + to_y % 4,
                        )
                    )
    return lax.ppermute(value, AXES, pairs)


def first_axis(step):
    return lambda z, c, x, y: (z, c, x + step, y) if c == 0 else (z, c, x, y + step)


def second_axis(step):
    return lambda z, c, x, y: (z, c, x, y + step) if c == 0 else (z, c, x + step, y)


def along_z(step):
    return lambda z, c, x, y: (z + step, c, x, y) if c == 0 else (z - step, c, x, y)


def other_core(z, c, x, y):
    return (z, 1 - c, x, y)


def product(left, right, m, rows):
    depth = left.shape[0] * 64
    pick = lambda plane: left[:, plane, :, pl.ds(m, rows)].reshape(depth, rows)
    take = lambda plane: right[:, plane].reshape(depth, 1024)
    dot = lambda a, b: lax.dot_general(
        a, b, (((0,), (0,)), ((), ())), preferred_element_type=jnp.float32
    )
    l0, l1, r0, r1 = pick(0), pick(1), take(0), take(1)
    return dot(l0, r0) - dot(l1, r1), dot(l0, r1) + dot(l1, r0)


def early_kernel(n_right, places, *refs):
    right_parts, left_parts = refs[:n_right], refs[n_right : n_right + 3]
    acc, last, left, right, sems = refs[n_right + 3 :]
    copies = []
    slot = 0
    for part in right_parts:
        for b in range(part.shape[0]):
            copies.append(
                pltpu.make_async_copy(part.at[b], right.at[places[slot]], sems.at[slot])
            )
            slot += 1
    for g, part in enumerate(left_parts):
        copies.append(
            pltpu.make_async_copy(part, left.at[pl.ds(4 * g, 4)], sems.at[slot + g])
        )
    for copy in copies:
        copy.start()
    for copy in copies:
        copy.wait()

    @pl.loop(0, 4)
    def _(t):
        m = pl.multiple_of(t * 256, 256)
        real, imag = product(left, right.at[pl.ds(0, 12)], m, 256)
        acc[0, pl.ds(m, 256)] = real
        acc[1, pl.ds(m, 256)] = imag

    last[...] = right[12:16]


def early(places, right_parts, left_parts):
    n = len(right_parts)
    anywhere = pl.BlockSpec(memory_space=pl.ANY)
    return pl.pallas_call(
        lambda *refs: early_kernel(n, *refs),
        out_shape=[
            pltpu.VMEM((2, 1024, 1024), jnp.float32),
            pltpu.VMEM((4, 2, 64, 1024), jnp.bfloat16),
        ],
        in_specs=[pl.BlockSpec(memory_space=pltpu.SMEM)] + [anywhere] * (n + 3),
        out_specs=[pl.BlockSpec(memory_space=pltpu.VMEM)] * 2,
        scratch_shapes=[
            pltpu.VMEM((12, 2, 64, 1024), jnp.bfloat16),
            pltpu.VMEM((16, 2, 64, 1024), jnp.bfloat16),
            pltpu.SemaphoreType.DMA((19,)),
        ],
        compiler_params=pltpu.CompilerParams(vmem_limit_bytes=40 * 2**20),
        cost_estimate=pl.CostEstimate(
            flops=6 * 2**30, bytes_accessed=8 * 2**20, transcendentals=0
        ),
    )(places, *right_parts, *left_parts)


def late_kernel(acc, right, left, out):
    m = pl.multiple_of(pl.program_id(0) * 128, 128)
    real, imag = product(left, right, m, 128)
    out[0] = acc[0, pl.ds(m, 128)] + real
    out[1] = acc[1, pl.ds(m, 128)] + imag


def late(acc, right, left):
    whole = pl.BlockSpec(memory_space=pltpu.VMEM)
    acc = pltpu.with_memory_space_constraint(acc, pltpu.VMEM)
    right = pltpu.with_memory_space_constraint(right, pltpu.VMEM)
    return pl.pallas_call(
        late_kernel,
        grid=(8,),
        out_shape=jax.ShapeDtypeStruct((2, 1024, 1024), jnp.float32),
        in_specs=[whole, whole, whole],
        out_specs=pl.BlockSpec((2, 128, 1024), lambda i: (0, i, 0)),
        compiler_params=pltpu.CompilerParams(vmem_limit_bytes=40 * 2**20),
        cost_estimate=pl.CostEstimate(
            flops=2 * 2**30, bytes_accessed=9 * 2**20, transcendentals=0
        ),
    )(acc, right, left)


def right_places():
    row, col = lax.axis_index("row"), lax.axis_index("col")
    z, core, x, y = row // 2, row % 2, col // 4, col % 4
    sign = 1 - 2 * core
    owners = []
    for far in range(4):
        for c in (core, 1 - core):
            owners.append((z - sign * far, c))
    owners.append((z - sign * 4, core))
    for far in range(1, 4):
        for c in (1 - core, core):
            owners.append((z + sign * far, c))
    owners.append((z - sign * 4, 1 - core))
    trace = jnp.stack([zz % 8 * 2 + c for zz, c in owners])
    dx, dy = (trace // 4 - x) % 4, (trace % 4 - y) % 4
    member = jnp.where(core == 0, dx, dy)
    group = jnp.where(core == 0, dy, dx)
    order = lambda d: jnp.where(d == 3, 1, jnp.where(d == 1, 2, jnp.where(d == 2, 3, 0)))
    return (order(group) * 4 + order(member)).astype(jnp.int32)


def local(left_panel, right_panel):
    own = jnp.swapaxes(left_panel, 1, 2)
    ring = jnp.stack([own] + [permute(own, first_axis(d)) for d in (1, -1, 2)])
    groups = [ring] + [permute(ring, second_axis(d)) for d in (1, -1, 2)]

    pair = jnp.stack([right_panel, permute(right_panel, other_core)])
    rights = [pair]
    for _ in range(3):
        rights.append(permute(rights[-1], along_z(1)))
    rights.append(permute(rights[-1][:1], along_z(1)))
    rights += [permute(part, other_core) for part in rights[1:]]

    acc, last = early(right_places(), rights, groups[:3])
    return late(acc, last, groups[3])


def solution(mesh):
    placed = (P(None, "row", "col"), P(None, "row", "col"))
    return jax.shard_map(
        local, mesh=mesh, in_specs=placed, out_specs=P(None, "row", "col"), check_vma=False
    )
```

```python
import jax
import jax.numpy as jnp
from jax import lax
from jax.experimental import pallas as pl
from jax.experimental.pallas import tpu as pltpu
from jax.sharding import PartitionSpec as P

AXES = ("row", "col")
RING = (0, -1, 1, 2)


def permute(value, target):
    pairs = []
    for z in range(8):
        for core in range(2):
            for x in range(4):
                for y in range(4):
                    to_z, to_core, to_x, to_y = target(z, core, x, y)
                    pairs.append(
                        (
                            (z * 2 + core) * 16 + x * 4 + y,
                            (to_z % 8 * 2 + to_core) * 16 + to_x % 4 * 4 + to_y % 4,
                        )
                    )
    return lax.ppermute(value, AXES, pairs)


def first_axis(step):
    return lambda z, c, x, y: (z, c, x + step, y) if c == 0 else (z, c, x, y + step)


def second_axis(step):
    return lambda z, c, x, y: (z, c, x, y + step) if c == 0 else (z, c, x + step, y)


def along_z(step):
    return lambda z, c, x, y: (z + step, c, x, y) if c == 0 else (z - step, c, x, y)


def other_core(z, c, x, y):
    return (z, 1 - c, x, y)


VMEM = pl.BlockSpec(memory_space=pltpu.VMEM)
SMEM = pl.BlockSpec(memory_space=pltpu.SMEM)
MIB = 2**20


def on_chip(*values):
    return [pltpu.with_memory_space_constraint(value, pltpu.VMEM) for value in values]


def limit(mib):
    return pltpu.CompilerParams(vmem_limit_bytes=mib * MIB)


def cost(flops, moved):
    return pl.CostEstimate(flops=flops, bytes_accessed=moved, transcendentals=0)


ANY = pl.BlockSpec(memory_space=pl.ANY)
HBM = pl.BlockSpec(memory_space=pltpu.HBM)
RIGHT = pltpu.VMEM((4, 2, 4, 64, 1024), jnp.bfloat16)


def in_hbm(value):
    return pltpu.with_memory_space_constraint(value, pltpu.HBM)


def slot_of(right, places, slot):
    at = places[slot]
    return right.at[at // 4, :, at % 4]


def stack_kernel(own, *refs):
    parts, out, sem = refs[:-2], refs[-2], refs[-1]
    copy = pltpu.make_async_copy(own, out.at[0], sem)
    copy.start()
    for i, part in enumerate(parts):
        out[i + 1] = part[...]
    copy.wait()


def stack(own, *parts):
    n = len(parts)
    return pl.pallas_call(
        stack_kernel,
        out_shape=pltpu.VMEM((n + 1, *own.shape), own.dtype),
        in_specs=[HBM] + [VMEM] * n,
        out_specs=VMEM,
        scratch_shapes=[pltpu.SemaphoreType.DMA],
        compiler_params=limit(2),
        cost_estimate=cost(0, 2 * MIB),
    )(in_hbm(own), *on_chip(*parts))


def first_kernel(places, mine, swapped, back, *refs):
    right, sem = refs[-2:]
    copy = pltpu.make_async_copy(mine, slot_of(right, places, 0), sem)
    copy.start()
    slot_of(right, places, 1)[...] = swapped[...]
    slot_of(right, places, 2)[...] = back[...]
    for slot in (FAR, FAR + 1):
        slot_of(right, places, slot)[...] = jnp.zeros((2, 64, 1024), jnp.bfloat16)
    copy.wait()


def first(places, mine, swapped, back, *others):
    return pl.pallas_call(
        first_kernel,
        out_shape=RIGHT,
        in_specs=[SMEM, HBM] + [VMEM] * 2 + [ANY] * len(others),
        out_specs=VMEM,
        scratch_shapes=[pltpu.SemaphoreType.DMA],
        compiler_params=limit(3),
        cost_estimate=cost(0, 2 * MIB),
    )(places, in_hbm(mine), *on_chip(swapped, back), *others)


def after(values, *others):
    n = len(values)
    return pl.pallas_call(
        lambda *refs: None,
        out_shape=[jax.ShapeDtypeStruct(v.shape, v.dtype) for v in values],
        in_specs=[ANY] * (n + len(others)),
        out_specs=[ANY] * n,
        input_output_aliases={i: i for i in range(n)},
        compiler_params=limit(1),
        cost_estimate=cost(0, 0),
    )(*values, *others)


def place_kernel(slots, places, *refs):
    right, sems = refs[-2:]
    copies = [
        pltpu.make_async_copy(part, slot_of(right, places, slot), sems.at[i])
        for i, (part, slot) in enumerate(zip(refs, slots))
    ]
    for copy in copies:
        copy.start()
    for copy in copies:
        copy.wait()


def place(right, slots, parts, places):
    n = len(parts)
    return pl.pallas_call(
        lambda *refs: place_kernel(slots, *refs),
        out_shape=RIGHT,
        in_specs=[SMEM] + [ANY] * (n + 1),
        out_specs=ANY,
        scratch_shapes=[pltpu.SemaphoreType.DMA((n,))],
        input_output_aliases={n + 1: 0},
        compiler_params=limit(1),
        cost_estimate=cost(0, MIB // 2),
    )(places, *parts, *on_chip(right))


def turned(left, rows):
    sides = []
    for plane in range(2):
        side = jnp.concatenate([part[:, plane, :, rows] for part in left])
        sides.append(side.reshape(side.shape[0] * 64, 256).T)
    return jnp.concatenate([sides[0], -sides[1]], 1), jnp.concatenate(sides[::-1], 1)


def turn_kernel(left, real, imag):
    for m in range(0, 1024, 256):
        rows = slice(m, m + 256)
        real[rows], imag[rows] = turned([left], rows)


def turn(left):
    out = pltpu.VMEM((1024, 512), jnp.bfloat16)
    return pl.pallas_call(
        turn_kernel,
        out_shape=[out, out],
        in_specs=[VMEM],
        out_specs=[VMEM] * 2,
        compiler_params=limit(6),
        cost_estimate=cost(0, 3 * MIB),
    )(*on_chip(left))


def early_kernel(right, *refs):
    reals, imags, acc = refs[0:6:2], refs[1:6:2], refs[6]

    @pl.loop(0, 4)
    def _(t):
        n = pl.ds(pl.multiple_of(t * 256, 256), 256)
        columns = right[0:3, :, :, :, n].reshape(1536, 256)
        for plane, sides in enumerate((reals, imags)):
            rows = jnp.concatenate([side[...] for side in sides], 1)
            acc[plane, :, n] = jnp.dot(rows, columns, preferred_element_type=jnp.float32)


def early(right, sides):
    return pl.pallas_call(
        early_kernel,
        out_shape=pltpu.VMEM((2, 1024, 1024), jnp.float32),
        in_specs=[VMEM] * 7,
        out_specs=VMEM,
        compiler_params=limit(8),
        cost_estimate=cost(6 * 2**30, 8 * MIB),
    )(*on_chip(right, *sides))


def late_kernel(places, acc, right, far_own, far_swapped, ring, back, ahead, up, down, out, extra):
    @pl.when(pl.program_id(0) == 0)
    def _():
        for i in range(2):
            at = places[14 + i]
            for g, group in enumerate((ring, back, ahead)):

                @pl.when(at // 4 == g)
                def _():
                    extra[i] = group[at % 4]

            @pl.when((at // 4 == 3) & (at % 4 < 2))
            def _():
                extra[i] = up[at % 2]

            @pl.when((at // 4 == 3) & (at % 4 >= 2))
            def _():
                extra[i] = down[at % 2]

    m = pl.ds(pl.multiple_of(pl.program_id(0) * 256, 256), 256)
    real, imag = turned([up, down, extra], m)
    columns = jnp.concatenate(
        [
            block
            for plane in range(2)
            for block in (right[3, plane].reshape(256, 1024), far_own[plane], far_swapped[plane])
        ]
    )
    out[0] = acc[0, m] + jnp.dot(real, columns, preferred_element_type=jnp.float32)
    out[1] = acc[1, m] + jnp.dot(imag, columns, preferred_element_type=jnp.float32)


def late(places, acc, right, far, groups, up, down):
    return pl.pallas_call(
        late_kernel,
        grid=(4,),
        out_shape=jax.ShapeDtypeStruct((2, 1024, 1024), jnp.float32),
        in_specs=[SMEM] + [VMEM] * 9,
        out_specs=pl.BlockSpec((2, 256, 1024), lambda i: (0, i, 0)),
        scratch_shapes=[pltpu.VMEM((2, 2, 64, 1024), jnp.bfloat16)],
        compiler_params=limit(14),
        cost_estimate=cost(3 * 2**30, 9 * MIB),
    )(places, *on_chip(acc, right, *far, *groups, up, down))


def right_places(offsets):
    row, col = lax.axis_index("row"), lax.axis_index("col")
    z, core, x, y = row // 2, row % 2, col // 4, col % 4
    sign = 1 - 2 * core
    trace = []
    for steps, shard, by in offsets:
        holder = core if by == 0 else 1 - core
        way = sign if by == 0 else -sign
        trace.append((z - way * steps) % 8 * 2 + (holder if shard == 0 else 1 - holder))
    trace = jnp.stack(trace)
    dx, dy = (trace // 4 - x) % 4, (trace % 4 - y) % 4
    member = jnp.where(core == 0, dx, dy)
    group = jnp.where(core == 0, dy, dx)
    order = lambda d: jnp.where(d == 3, 1, jnp.where(d == 1, 2, jnp.where(d == 2, 3, 0)))
    return (order(group) * 4 + order(member)).astype(jnp.int32)


BLOCKS = [(0, 0, 0), (0, 1, 0)]
BLOCKS += [(step, shard, by) for step in range(1, 4) for shard in range(2) for by in range(2)]
BLOCKS += [(4, 0, 0), (4, 0, 1)]
FAR = 14


def local(left_panel, right_panel):
    own = jnp.swapaxes(left_panel, 1, 2)
    places = right_places(BLOCKS)
    swapped = permute(right_panel, other_core)
    near = [permute(own, first_axis(d)) for d in (1, -1, 2)]
    ring = stack(own, *near)
    back = permute(ring, second_axis(1))
    ahead = permute(ring, second_axis(-1))
    far_back = permute(back[:2], second_axis(1))
    far_ahead = permute(ahead[2:], second_axis(-1))

    held = [right_panel, swapped]
    waiting = []
    for slot in range(2, FAR, 2):
        step, shard, _ = BLOCKS[slot]
        part = permute(held[shard], along_z(1))
        if slot == 2:
            right = first(places, right_panel, swapped, part, ring)
        else:
            due = waiting[:1] if slot < 12 else waiting[:1]
            waiting = waiting[1:]
            right = place(right, [slot] + [s for s, _ in due], [part] + [p for _, p in due], places)
        part, = after((part,), right)
        held[shard] = part
        waiting.append((slot + 1, permute(part, other_core)))
    far = permute(held[0], along_z(1))
    right = place(right, [s for s, _ in waiting], [p for _, p in waiting], places)

    groups = (ring, back, ahead)
    acc = early(right, [side for group in groups for side in turn(group)])
    far, = after((far,), acc)
    return late(places, acc, right, (far, permute(far, other_core)), groups, far_back, far_ahead)


def solution(mesh):
    placed = (P(None, "row", "col"), P(None, "row", "col"))
    return jax.shard_map(
        local, mesh=mesh, in_specs=placed, out_specs=P(None, "row", "col"), check_vma=False
    )
```

```python
import jax
import jax.numpy as jnp
from jax import lax
from jax.experimental import pallas as pl
from jax.experimental.pallas import tpu as pltpu
from jax.sharding import PartitionSpec as P

AXES = ("row", "col")
RING = (0, -1, 1, 2)


def permute(value, target):
    pairs = []
    for z in range(8):
        for core in range(2):
            for x in range(4):
                for y in range(4):
                    to_z, to_core, to_x, to_y = target(z, core, x, y)
                    pairs.append(
                        (
                            (z * 2 + core) * 16 + x * 4 + y,
                            (to_z % 8 * 2 + to_core) * 16 + to_x % 4 * 4 + to_y % 4,
                        )
                    )
    return lax.ppermute(value, AXES, pairs)


def first_axis(step):
    return lambda z, c, x, y: (z, c, x + step, y) if c == 0 else (z, c, x, y + step)


def second_axis(step):
    return lambda z, c, x, y: (z, c, x, y + step) if c == 0 else (z, c, x + step, y)


def along_z(step):
    return lambda z, c, x, y: (z + step, c, x, y) if c == 0 else (z - step, c, x, y)


def other_core(z, c, x, y):
    return (z, 1 - c, x, y)


VMEM = pl.BlockSpec(memory_space=pltpu.VMEM)
SMEM = pl.BlockSpec(memory_space=pltpu.SMEM)
MIB = 2**20


def on_chip(*values):
    return [pltpu.with_memory_space_constraint(value, pltpu.VMEM) for value in values]


def limit(mib):
    return pltpu.CompilerParams(vmem_limit_bytes=mib * MIB)


def cost(flops, moved):
    return pl.CostEstimate(flops=flops, bytes_accessed=moved, transcendentals=0)


ANY = pl.BlockSpec(memory_space=pl.ANY)
HBM = pl.BlockSpec(memory_space=pltpu.HBM)
RIGHT = pltpu.VMEM((4, 2, 4, 64, 1024), jnp.bfloat16)


def in_hbm(value):
    return pltpu.with_memory_space_constraint(value, pltpu.HBM)


def slot_of(right, places, slot):
    at = places[slot]
    return right.at[at // 4, :, at % 4]


def stack_kernel(own, *refs):
    parts, out, sem = refs[:-2], refs[-2], refs[-1]
    copy = pltpu.make_async_copy(own, out.at[0], sem)
    copy.start()
    for i, part in enumerate(parts):
        out[i + 1] = part[...]
    copy.wait()


def stack(own, *parts):
    n = len(parts)
    return pl.pallas_call(
        stack_kernel,
        out_shape=pltpu.VMEM((n + 1, *own.shape), own.dtype),
        in_specs=[HBM] + [VMEM] * n,
        out_specs=VMEM,
        scratch_shapes=[pltpu.SemaphoreType.DMA],
        compiler_params=limit(2),
        cost_estimate=cost(0, 2 * MIB),
    )(in_hbm(own), *on_chip(*parts))


def first_kernel(places, mine, swapped, back, *refs):
    right, sem = refs[-2:]
    copy = pltpu.make_async_copy(mine, slot_of(right, places, 0), sem)
    copy.start()
    slot_of(right, places, 1)[...] = swapped[...]
    slot_of(right, places, 2)[...] = back[...]
    for slot in (FAR, FAR + 1):
        slot_of(right, places, slot)[...] = jnp.zeros((2, 64, 1024), jnp.bfloat16)
    copy.wait()


def first(places, mine, swapped, back, *others):
    return pl.pallas_call(
        first_kernel,
        out_shape=RIGHT,
        in_specs=[SMEM, HBM] + [VMEM] * 2 + [ANY] * len(others),
        out_specs=VMEM,
        scratch_shapes=[pltpu.SemaphoreType.DMA],
        compiler_params=limit(3),
        cost_estimate=cost(0, 2 * MIB),
    )(places, in_hbm(mine), *on_chip(swapped, back), *others)


def after(values, *others):
    n = len(values)
    return pl.pallas_call(
        lambda *refs: None,
        out_shape=[jax.ShapeDtypeStruct(v.shape, v.dtype) for v in values],
        in_specs=[ANY] * (n + len(others)),
        out_specs=[ANY] * n,
        input_output_aliases={i: i for i in range(n)},
        compiler_params=limit(1),
        cost_estimate=cost(0, 0),
    )(*values, *others)


def place_kernel(slots, places, *refs):
    right, sems = refs[-2:]
    copies = [
        pltpu.make_async_copy(part, slot_of(right, places, slot), sems.at[i])
        for i, (part, slot) in enumerate(zip(refs, slots))
    ]
    for copy in copies:
        copy.start()
    for copy in copies:
        copy.wait()


def place(right, slots, parts, places):
    n = len(parts)
    return pl.pallas_call(
        lambda *refs: place_kernel(slots, *refs),
        out_shape=RIGHT,
        in_specs=[SMEM] + [ANY] * (n + 1),
        out_specs=ANY,
        scratch_shapes=[pltpu.SemaphoreType.DMA((n,))],
        input_output_aliases={n + 1: 0},
        compiler_params=limit(1),
        cost_estimate=cost(0, MIB // 2),
    )(places, *parts, *on_chip(right))


def turned(left, rows):
    sides = []
    for plane in range(2):
        side = jnp.concatenate([part[:, plane, :, rows] for part in left])
        sides.append(side.reshape(side.shape[0] * 64, 256).T)
    return jnp.concatenate([sides[0], -sides[1]], 1), jnp.concatenate(sides[::-1], 1)


def turn_kernel(left, real, imag):
    for m in range(0, 1024, 256):
        rows = slice(m, m + 256)
        real[rows], imag[rows] = turned([left], rows)


def turn(left):
    out = pltpu.VMEM((1024, 512), jnp.bfloat16)
    return pl.pallas_call(
        turn_kernel,
        out_shape=[out, out],
        in_specs=[VMEM],
        out_specs=[VMEM] * 2,
        compiler_params=limit(6),
        cost_estimate=cost(0, 3 * MIB),
    )(*on_chip(left))


def early_kernel(right, *refs):
    reals, imags, acc = refs[0:6:2], refs[1:6:2], refs[6]

    @pl.loop(0, 4)
    def _(t):
        n = pl.ds(pl.multiple_of(t * 256, 256), 256)
        columns = right[0:3, :, :, :, n].reshape(1536, 256)
        for plane, sides in enumerate((reals, imags)):
            rows = jnp.concatenate([side[...] for side in sides], 1)
            acc[plane, :, n] = jnp.dot(rows, columns, preferred_element_type=jnp.float32)


def early(right, sides):
    return pl.pallas_call(
        early_kernel,
        out_shape=pltpu.VMEM((2, 1024, 1024), jnp.float32),
        in_specs=[VMEM] * 7,
        out_specs=VMEM,
        compiler_params=limit(8),
        cost_estimate=cost(6 * 2**30, 8 * MIB),
    )(*on_chip(right, *sides))


def late_kernel(places, acc, right, far_own, far_swapped, ring, back, ahead, up, down, out, extra):
    @pl.when(pl.program_id(0) == 0)
    def _():
        for i in range(2):
            at = places[14 + i]
            for g, group in enumerate((ring, back, ahead)):

                @pl.when(at // 4 == g)
                def _():
                    extra[i] = group[at % 4]

            @pl.when((at // 4 == 3) & (at % 4 < 2))
            def _():
                extra[i] = up[at % 2]

            @pl.when((at // 4 == 3) & (at % 4 >= 2))
            def _():
                extra[i] = down[at % 2]

    m = pl.ds(pl.multiple_of(pl.program_id(0) * 256, 256), 256)
    real, imag = turned([up, down, extra], m)
    columns = jnp.concatenate(
        [
            block
            for plane in range(2)
            for block in (right[3, plane].reshape(256, 1024), far_own[plane], far_swapped[plane])
        ]
    )
    out[0] = acc[0, m] + jnp.dot(real, columns, preferred_element_type=jnp.float32)
    out[1] = acc[1, m] + jnp.dot(imag, columns, preferred_element_type=jnp.float32)


def late(places, acc, right, far, groups, up, down):
    return pl.pallas_call(
        late_kernel,
        grid=(4,),
        out_shape=jax.ShapeDtypeStruct((2, 1024, 1024), jnp.float32),
        in_specs=[SMEM] + [VMEM] * 9,
        out_specs=pl.BlockSpec((2, 256, 1024), lambda i: (0, i, 0)),
        scratch_shapes=[pltpu.VMEM((2, 2, 64, 1024), jnp.bfloat16)],
        compiler_params=limit(14),
        cost_estimate=cost(3 * 2**30, 9 * MIB),
    )(places, *on_chip(acc, right, *far, *groups, up, down))


def right_places(offsets):
    row, col = lax.axis_index("row"), lax.axis_index("col")
    z, core, x, y = row // 2, row % 2, col // 4, col % 4
    sign = 1 - 2 * core
    trace = []
    for steps, shard, by in offsets:
        holder = core if by == 0 else 1 - core
        way = sign if by == 0 else -sign
        trace.append((z - way * steps) % 8 * 2 + (holder if shard == 0 else 1 - holder))
    trace = jnp.stack(trace)
    dx, dy = (trace // 4 - x) % 4, (trace % 4 - y) % 4
    member = jnp.where(core == 0, dx, dy)
    group = jnp.where(core == 0, dy, dx)
    order = lambda d: jnp.where(d == 3, 1, jnp.where(d == 1, 2, jnp.where(d == 2, 3, 0)))
    return (order(group) * 4 + order(member)).astype(jnp.int32)


BLOCKS = [(0, 0, 0), (0, 1, 0)]
BLOCKS += [(step, shard, by) for step in range(1, 4) for shard in range(2) for by in range(2)]
BLOCKS += [(4, 0, 0), (4, 0, 1)]
FAR = 14


def local(left_panel, right_panel):
    own = jnp.swapaxes(left_panel, 1, 2)
    places = right_places(BLOCKS)
    swapped = permute(right_panel, other_core)
    near = [permute(own, first_axis(d)) for d in (1, -1, 2)]
    ring = stack(own, *near)
    back = permute(ring, second_axis(1))
    ahead = permute(ring, second_axis(-1))
    far_back = permute(back[:2], second_axis(1))
    far_ahead = permute(ahead[2:], second_axis(-1))

    sides = []
    held = [right_panel, swapped]
    waiting = []
    for slot in range(2, FAR, 2):
        step, shard, _ = BLOCKS[slot]
        part = permute(held[shard], along_z(1))
        if slot == 2:
            right = first(places, right_panel, swapped, part, ring)
        else:
            due = waiting[:1] if slot < 12 else waiting[:1]
            waiting = waiting[1:]
            right = place(right, [slot] + [s for s, _ in due], [part] + [p for _, p in due], places)
        others = {10: (back, ahead), 12: [s for side in sides for s in side]}.get(slot, ())
        if slot == 10:
            sides = [turn(group) for group in (ring, back, ahead)]
        part, = after((part,), right, *others)
        held[shard] = part
        waiting.append((slot + 1, permute(part, other_core)))
    far = permute(held[0], along_z(1))
    right = place(right, [s for s, _ in waiting], [p for _, p in waiting], places)

    groups = (ring, back, ahead)
    acc = early(right, [s for side in sides for s in side])
    far, = after((far,), acc)
    return late(places, acc, right, (far, permute(far, other_core)), groups, far_back, far_ahead)


def solution(mesh):
    placed = (P(None, "row", "col"), P(None, "row", "col"))
    return jax.shard_map(
        local, mesh=mesh, in_specs=placed, out_specs=P(None, "row", "col"), check_vma=False
    )
```

```python
import jax
import jax.numpy as jnp
from jax import lax
from jax.experimental import pallas as pl
from jax.experimental.pallas import tpu as pltpu
from jax.sharding import PartitionSpec as P

AXES = ("row", "col")
RING = (0, -1, 1, 2)


def permute(value, target):
    pairs = []
    for z in range(8):
        for core in range(2):
            for x in range(4):
                for y in range(4):
                    to_z, to_core, to_x, to_y = target(z, core, x, y)
                    pairs.append(
                        (
                            (z * 2 + core) * 16 + x * 4 + y,
                            (to_z % 8 * 2 + to_core) * 16 + to_x % 4 * 4 + to_y % 4,
                        )
                    )
    return lax.ppermute(value, AXES, pairs)


def first_axis(step):
    return lambda z, c, x, y: (z, c, x + step, y) if c == 0 else (z, c, x, y + step)


def second_axis(step):
    return lambda z, c, x, y: (z, c, x, y + step) if c == 0 else (z, c, x + step, y)


def along_z(step):
    return lambda z, c, x, y: (z + step, c, x, y) if c == 0 else (z - step, c, x, y)


def other_core(z, c, x, y):
    return (z, 1 - c, x, y)


VMEM = pl.BlockSpec(memory_space=pltpu.VMEM)
SMEM = pl.BlockSpec(memory_space=pltpu.SMEM)
MIB = 2**20


def on_chip(*values):
    return [pltpu.with_memory_space_constraint(value, pltpu.VMEM) for value in values]


def limit(mib):
    return pltpu.CompilerParams(vmem_limit_bytes=mib * MIB)


def cost(flops, moved):
    return pl.CostEstimate(flops=flops, bytes_accessed=moved, transcendentals=0)


ANY = pl.BlockSpec(memory_space=pl.ANY)
HBM = pl.BlockSpec(memory_space=pltpu.HBM)
RIGHT = pltpu.VMEM((4, 2, 4, 64, 1024), jnp.bfloat16)


def in_hbm(value):
    return pltpu.with_memory_space_constraint(value, pltpu.HBM)


def slot_of(right, places, slot):
    at = places[slot]
    return right.at[at // 4, :, at % 4]


def stack_kernel(own, *refs):
    parts, out, sem = refs[:-2], refs[-2], refs[-1]
    copy = pltpu.make_async_copy(own, out.at[0], sem)
    copy.start()
    for i, part in enumerate(parts):
        out[i + 1] = part[...]
    copy.wait()


def stack(own, *parts):
    n = len(parts)
    return pl.pallas_call(
        stack_kernel,
        out_shape=pltpu.VMEM((n + 1, *own.shape), own.dtype),
        in_specs=[HBM] + [VMEM] * n,
        out_specs=VMEM,
        scratch_shapes=[pltpu.SemaphoreType.DMA],
        compiler_params=limit(2),
        cost_estimate=cost(0, 2 * MIB),
    )(in_hbm(own), *on_chip(*parts))


def first_kernel(places, swapped, back, *refs):
    right = refs[-1]
    slot_of(right, places, 1)[...] = swapped[...]
    slot_of(right, places, 2)[...] = back[...]
    for slot in (FAR, FAR + 1):
        slot_of(right, places, slot)[...] = jnp.zeros((2, 64, 1024), jnp.bfloat16)


def first(places, swapped, back, *others):
    return pl.pallas_call(
        first_kernel,
        out_shape=RIGHT,
        in_specs=[SMEM] + [VMEM] * 2 + [ANY] * len(others),
        out_specs=VMEM,
        compiler_params=limit(3),
        cost_estimate=cost(0, 2 * MIB),
    )(places, *on_chip(swapped, back), *others)


def after(values, *others):
    n = len(values)
    return pl.pallas_call(
        lambda *refs: None,
        out_shape=[jax.ShapeDtypeStruct(v.shape, v.dtype) for v in values],
        in_specs=[ANY] * (n + len(others)),
        out_specs=[ANY] * n,
        input_output_aliases={i: i for i in range(n)},
        compiler_params=limit(1),
        cost_estimate=cost(0, 0),
    )(*values, *others)


def place_kernel(slots, places, *refs):
    right, sems = refs[-2:]
    copies = [
        pltpu.make_async_copy(part, slot_of(right, places, slot), sems.at[i])
        for i, (part, slot) in enumerate(zip(refs, slots))
    ]
    for copy in copies:
        copy.start()
    for copy in copies:
        copy.wait()


def place(right, slots, parts, places):
    n = len(parts)
    return pl.pallas_call(
        lambda *refs: place_kernel(slots, *refs),
        out_shape=RIGHT,
        in_specs=[SMEM] + [ANY] * (n + 1),
        out_specs=ANY,
        scratch_shapes=[pltpu.SemaphoreType.DMA((n,))],
        input_output_aliases={n + 1: 0},
        compiler_params=limit(1),
        cost_estimate=cost(0, MIB // 2),
    )(places, *parts, *on_chip(right))


def turned(left, rows):
    sides = []
    for plane in range(2):
        side = jnp.concatenate([part[:, plane, :, rows] for part in left])
        sides.append(side.reshape(side.shape[0] * 64, 256).T)
    return jnp.concatenate([sides[0], -sides[1]], 1), jnp.concatenate(sides[::-1], 1)


def turn_kernel(left, real, imag):
    for m in range(0, 1024, 256):
        rows = slice(m, m + 256)
        real[rows], imag[rows] = turned([left], rows)


def turn(left):
    out = pltpu.VMEM((1024, 512), jnp.bfloat16)
    return pl.pallas_call(
        turn_kernel,
        out_shape=[out, out],
        in_specs=[VMEM],
        out_specs=[VMEM] * 2,
        compiler_params=limit(6),
        cost_estimate=cost(0, 3 * MIB),
    )(*on_chip(left))


def early_kernel(right, *refs):
    reals, imags, acc = refs[0:6:2], refs[1:6:2], refs[6]

    @pl.loop(0, 4)
    def _(t):
        n = pl.ds(pl.multiple_of(t * 256, 256), 256)
        columns = right[0:3, :, :, :, n].reshape(1536, 256)
        for plane, sides in enumerate((reals, imags)):
            rows = jnp.concatenate([side[...] for side in sides], 1)
            acc[plane, :, n] = jnp.dot(rows, columns, preferred_element_type=jnp.float32)


def early(right, sides):
    return pl.pallas_call(
        early_kernel,
        out_shape=pltpu.VMEM((2, 1024, 1024), jnp.float32),
        in_specs=[VMEM] * 7,
        out_specs=VMEM,
        compiler_params=limit(8),
        cost_estimate=cost(6 * 2**30, 8 * MIB),
    )(*on_chip(right, *sides))


def late_kernel(places, acc, right, far_own, far_swapped, ring, back, ahead, up, down, out, extra):
    @pl.when(pl.program_id(0) == 0)
    def _():
        for i in range(2):
            at = places[14 + i]
            for g, group in enumerate((ring, back, ahead)):

                @pl.when(at // 4 == g)
                def _():
                    extra[i] = group[at % 4]

            @pl.when((at // 4 == 3) & (at % 4 < 2))
            def _():
                extra[i] = up[at % 2]

            @pl.when((at // 4 == 3) & (at % 4 >= 2))
            def _():
                extra[i] = down[at % 2]

    m = pl.ds(pl.multiple_of(pl.program_id(0) * 256, 256), 256)
    real, imag = turned([up, down, extra], m)
    columns = jnp.concatenate(
        [
            block
            for plane in range(2)
            for block in (right[3, plane].reshape(256, 1024), far_own[plane], far_swapped[plane])
        ]
    )
    out[0] = acc[0, m] + jnp.dot(real, columns, preferred_element_type=jnp.float32)
    out[1] = acc[1, m] + jnp.dot(imag, columns, preferred_element_type=jnp.float32)


def late(places, acc, right, far, groups, up, down):
    return pl.pallas_call(
        late_kernel,
        grid=(4,),
        out_shape=jax.ShapeDtypeStruct((2, 1024, 1024), jnp.float32),
        in_specs=[SMEM] + [VMEM] * 9,
        out_specs=pl.BlockSpec((2, 256, 1024), lambda i: (0, i, 0)),
        scratch_shapes=[pltpu.VMEM((2, 2, 64, 1024), jnp.bfloat16)],
        compiler_params=limit(14),
        cost_estimate=cost(3 * 2**30, 9 * MIB),
    )(places, *on_chip(acc, right, *far, *groups, up, down))


def right_places(offsets):
    row, col = lax.axis_index("row"), lax.axis_index("col")
    z, core, x, y = row // 2, row % 2, col // 4, col % 4
    sign = 1 - 2 * core
    trace = []
    for steps, shard, by in offsets:
        holder = core if by == 0 else 1 - core
        way = sign if by == 0 else -sign
        trace.append((z - way * steps) % 8 * 2 + (holder if shard == 0 else 1 - holder))
    trace = jnp.stack(trace)
    dx, dy = (trace // 4 - x) % 4, (trace % 4 - y) % 4
    member = jnp.where(core == 0, dx, dy)
    group = jnp.where(core == 0, dy, dx)
    order = lambda d: jnp.where(d == 3, 1, jnp.where(d == 1, 2, jnp.where(d == 2, 3, 0)))
    return (order(group) * 4 + order(member)).astype(jnp.int32)


BLOCKS = [(0, 0, 0), (0, 1, 0)]
BLOCKS += [(step, shard, by) for step in range(1, 4) for shard in range(2) for by in range(2)]
BLOCKS += [(4, 0, 0), (4, 0, 1)]
FAR = 14


def local(left_panel, right_panel):
    own = jnp.swapaxes(left_panel, 1, 2)
    places = right_places(BLOCKS)
    swapped = permute(right_panel, other_core)
    near = [permute(own, first_axis(d)) for d in (1, -1, 2)]
    ring = stack(own, *near)
    back = permute(ring, second_axis(1))
    ahead = permute(ring, second_axis(-1))
    far_back = permute(back[:2], second_axis(1))
    far_ahead = permute(ahead[2:], second_axis(-1))

    sides = []
    held = [right_panel, swapped]
    waiting = [(0, in_hbm(right_panel))]
    for slot in range(2, FAR, 2):
        step, shard, _ = BLOCKS[slot]
        part = permute(held[shard], along_z(1))
        if slot == 2:
            right = first(places, swapped, part, ring)
        else:
            count = 2 if slot == 4 else 1
            due, waiting = waiting[:count], waiting[count:]
            right = place(right, [slot] + [s for s, _ in due], [part] + [p for _, p in due], places)
        others = {10: (back, ahead), 12: [s for side in sides for s in side]}.get(slot, ())
        if slot == 10:
            sides = [turn(group) for group in (ring, back, ahead)]
        part, = after((part,), right, *others)
        held[shard] = part
        waiting.append((slot + 1, permute(part, other_core)))
    far = permute(held[0], along_z(1))
    right = place(right, [s for s, _ in waiting], [p for _, p in waiting], places)

    groups = (ring, back, ahead)
    acc = early(right, [s for side in sides for s in side])
    far, = after((far,), acc)
    return late(places, acc, right, (far, permute(far, other_core)), groups, far_back, far_ahead)


def solution(mesh):
    placed = (P(None, "row", "col"), P(None, "row", "col"))
    return jax.shard_map(
        local, mesh=mesh, in_specs=placed, out_specs=P(None, "row", "col"), check_vma=False
    )
```
